256 devices in a mesh: tile: 64 (over y, z, core), mem: 4 (over x).
Axes of the slice: x: 4, y: 4, z: 8, core: 2. Of those that a mesh axis runs over, the one named last changes fastest.
Arguments:
- ensemble: float32 [64, 4, 24, 128, 256], P('mem', None, None, 'tile'), may hold values from -6 to 6
- courant: float32 [2, 24, 128, 256], P(None, None, 'tile'), may hold values from -0.5 to 0.5
- diffusion: float32 [4, 24], replicated, may hold values from 0.02 to 0.2
- observation_row: int32 [256], replicated, may hold values from 0 to 127
- observation_column: int32 [256], replicated, may hold values from 0 to 255
- observation_field: int32 [256], replicated, may hold values from 0 to 3
- observation_level: int32 [256], replicated, may hold values from 0 to 23
- obs_value: float32 [256], replicated, may hold values from -6 to 6
- obs_error: float32 [256], replicated, may hold values from 0.2 to 2
- localize: float32 [64, 256], replicated, may hold values from 0 to 1
Outputs:
- analysis: float32 [64, 4, 24, 128, 256], P('mem', None, None, 'tile')
The draws below stay inside these ranges and needn't reach their ends.
All inputs are finite; a program needn't handle non-finite values.
Results may differ from the reference program's by a relative error of at most 0.00013.
Values sent between devices are 32-bit elements; how exact they have to be, the bound alone decides.
No kernel may reach another device: no remote copies, remote signals or barrier semaphores. Data moves between devices by JAX's collectives and lax.ppermute only.
A program may use at most 128 MiB of HBM per device.

```python
import math
import jax
import jax.numpy as jnp
from jax import lax

ROWS_DEV = 2
NY = 256
FIELDS = 4
LEV = 24
BATCH = 128
STEPS = 2
ENS = 64
NX = 128
NOBS = 256
N_TILE = 64


def set_ends(values, rng, low, largest):
    longest = values.shape.index(max(values.shape))
    spots = []
    for shift in (0, 1):
        where = [jax.random.randint(jax.random.fold_in(rng, axis), (), 0, length) for axis, length in enumerate(values.shape)]
        where[longest] = (where[longest] + shift) % values.shape[longest]
        spots.append(tuple(where))
    return values.at[spots[0]].set(low).at[spots[1]].set(largest)


def level_of(own_key, extent, shards, smallest, top_value):
    def one(dim, blocks):
        draws = jax.random.uniform(jax.random.fold_in(jax.random.fold_in(own_key, 6), dim), (blocks,), jnp.float32, smallest / len(shards), top_value / len(shards))
        return jnp.repeat(jnp.exp(draws), extent[dim] // blocks).reshape((-1,) + (1,) * (len(extent) - dim - 1))

    factor_of = one(*shards[0])
    for cut in shards[1:]:
        factor_of = factor_of * one(*cut)
    return factor_of


def centred(rng, extent, deviation, bound, split=(), kind=jnp.bfloat16):
    gain = level_of(rng, extent, split, -0.22, 0.18) if split else 1.0
    entries = jax.random.normal(rng, extent, jnp.float32) * deviation * gain
    return jnp.minimum(jnp.maximum(entries, -bound), bound).astype(kind)


def setup_inputs(seed: int = 0) -> dict:
    key_of = jax.random.split(jax.random.key(seed), 11)
    ensemble = centred(key_of[0], (ENS, FIELDS, LEV, NX, NY), 1.0, 6.0, ((0, 4), (3, 64)), jnp.float32)
    courant = jnp.clip(jax.random.uniform(key_of[1], (2, LEV, NX, NY), jnp.float32, -0.5, 0.5) * level_of(key_of[1], (2, LEV, NX, NY), ((2, 64),), -0.4, 0.0), -0.5, 0.5)
    diffusion = jnp.clip(jnp.exp(jax.random.uniform(key_of[2], (FIELDS, LEV), jnp.float32, math.log(0.02), math.log(0.2))), 0.02, 0.2)
    observation_row = set_ends(jax.random.randint(key_of[3], (NOBS,), 0, NX), jax.random.fold_in(key_of[3], 1), 0, NX - 1).astype(jnp.int32)
    observation_column = set_ends(jax.random.randint(key_of[4], (NOBS,), 0, NY), jax.random.fold_in(key_of[4], 1), 0, NY - 1).astype(jnp.int32)
    observation_field = set_ends(jax.random.randint(key_of[5], (NOBS,), 0, FIELDS), jax.random.fold_in(key_of[5], 1), 0, FIELDS - 1).astype(jnp.int32)
    observation_level = set_ends(jax.random.randint(key_of[6], (NOBS,), 0, LEV), jax.random.fold_in(key_of[6], 1), 0, LEV - 1).astype(jnp.int32)
    obs_value = centred(key_of[7], (NOBS,), 1.0, 6.0, (), jnp.float32)
    obs_error = jnp.clip(jnp.exp(jax.random.uniform(key_of[8], (NOBS,), jnp.float32, math.log(0.2), math.log(2.0))), 0.2, 2.0)
    localize = jnp.clip(jax.random.uniform(key_of[9], (N_TILE, NOBS), jnp.float32, 0.0, 1.0), 0.0, 1.0)
    return {"ensemble": ensemble, "courant": courant, "diffusion": diffusion, "observation_row": observation_row, "observation_column": observation_column, "observation_field": observation_field, "observation_level": observation_level, "obs_value": obs_value, "obs_error": obs_error, "localize": localize}


def advance(extended, courant, diffusion):
    centre = extended[..., 2:-2, :]
    up_one = extended[..., 3:-1, :]
    down_one = extended[..., 1:-3, :]
    up_two = extended[..., 4:, :]
    down_two = extended[..., :-4, :]
    right_one = jnp.roll(centre, -1, axis=-1)
    left_one = jnp.roll(centre, 1, axis=-1)
    right_two = jnp.roll(centre, -2, axis=-1)
    left_two = jnp.roll(centre, 2, axis=-1)
    slope_rows = (8.0 * (up_one - down_one) - (up_two - down_two)) / 12.0
    slope_cols = (8.0 * (right_one - left_one) - (right_two - left_two)) / 12.0
    spread = up_one + down_one + right_one + left_one - 4.0 * centre
    return centre - courant[0] * slope_rows - courant[1] * slope_cols + diffusion[:, :, None, None] * spread

def assimilate(prior, values, errors, row_weights, tile_weights):
    members = prior.shape[1]
    start = jnp.broadcast_to(jnp.eye(members, dtype=jnp.float32), (tile_weights.shape[0], members, members))

    def one_obs(position, state_pair):
        priors, transform = state_pair
        sample = lax.dynamic_index_in_dim(priors, position, 0, keepdims=False)
        centre = jnp.mean(sample)
        anomaly = sample - centre
        variance = jnp.sum(anomaly * anomaly) / (members - 1.0)
        obs_err = lax.dynamic_index_in_dim(errors, position, 0, keepdims=False)
        target = lax.dynamic_index_in_dim(values, position, 0, keepdims=False)
        spread_sum = variance + obs_err
        shrink = 1.0 / (1.0 + jnp.sqrt(obs_err / spread_sum))
        increment = (target - centre - shrink * anomaly) / spread_sum
        scaled = anomaly / (members - 1.0)
        projected = jnp.dot(priors, scaled, precision=lax.Precision.HIGHEST)
        weight_rows = lax.dynamic_index_in_dim(row_weights, position, 1, keepdims=False)
        priors = priors + (weight_rows * projected)[:, None] * increment[None, :]
        pushed = jnp.einsum('tab,b->ta', transform, scaled, precision=lax.Precision.HIGHEST)
        weight_tiles = lax.dynamic_index_in_dim(tile_weights, position, 1, keepdims=False)
        transform = transform + weight_tiles[:, None, None] * pushed[:, :, None] * increment[None, None, :]
        return (priors, transform)
    return lax.fori_loop(0, prior.shape[0], one_obs, (prior, start), unroll=8)[1]

def reference(ensemble, courant, diffusion, observation_row, observation_column, observation_field, observation_level, obs_value, obs_error, localize):

    def predicted_member(ensemble_member):
        for step_count in range(STEPS):
            extended = jnp.concatenate([ensemble_member[..., -2:, :], ensemble_member, ensemble_member[..., :2, :]], axis=-2)
            ensemble_member = advance(extended, courant, diffusion)
        return ensemble_member
    predicted_state = lax.map(predicted_member, ensemble)
    unprocessed_state = predicted_state[:, observation_field, observation_level, observation_row, observation_column].T
    owner = observation_row // ROWS_DEV
    tiles = localize.shape[0]
    owner_hot = (owner[:, None] == jnp.arange(tiles, dtype=jnp.int32)[None, :]).astype(jnp.float32)
    row_weights = jnp.dot(owner_hot, localize, precision=lax.Precision.HIGHEST)
    leading_part = assimilate(unprocessed_state[:BATCH], obs_value[:BATCH], obs_error[:BATCH], row_weights[:BATCH, :BATCH], localize[:, :BATCH])
    picked = jnp.einsum('kt,tef->kef', owner_hot[BATCH:], leading_part, precision=lax.Precision.HIGHEST)
    second_prior = jnp.einsum('ke,kef->kf', unprocessed_state[BATCH:], picked, precision=lax.Precision.HIGHEST)
    trailing_part = assimilate(second_prior, obs_value[BATCH:], obs_error[BATCH:], row_weights[BATCH:, BATCH:], localize[:, BATCH:])
    joined_result = jnp.einsum('srx,sxf->srf', leading_part, trailing_part, precision=lax.Precision.HIGHEST)
    each_row_count = jnp.repeat(joined_result, ROWS_DEV, axis=0)
    return jnp.einsum('btkeo,ebc->ctkeo', predicted_state, each_row_count, precision=lax.Precision.HIGHEST)
```

```python
import functools

import jax
import jax.numpy as jnp
from jax import lax
from jax.experimental import pallas as pl
from jax.experimental.pallas import tpu as pltpu
from jax.sharding import PartitionSpec as P

STEPS = 2


def padded(cells, sides, width):
    for axis, dim in sides:
        count = lax.axis_size(axis)
        head = lax.slice_in_dim(cells, 0, width, axis=dim)
        tail = lax.slice_in_dim(cells, cells.shape[dim] - width, cells.shape[dim], axis=dim)
        cells = jnp.concatenate(
            [
                lax.ppermute(tail, axis, [(i, (i + 1) % count) for i in range(count)]),
                cells,
                lax.ppermute(head, axis, [((i + 1) % count, i) for i in range(count)]),
            ],
            axis=dim,
        )
    return cells


def advance(extended, courant, diffusion):
    centre = extended[..., 2:-2, :]
    up_one = extended[..., 3:-1, :]
    down_one = extended[..., 1:-3, :]
    up_two = extended[..., 4:, :]
    down_two = extended[..., :-4, :]
    right_one = jnp.roll(centre, -1, axis=-1)
    left_one = jnp.roll(centre, 1, axis=-1)
    right_two = jnp.roll(centre, -2, axis=-1)
    left_two = jnp.roll(centre, 2, axis=-1)
    slope_rows = (8.0 * (up_one - down_one) - (up_two - down_two)) / 12.0
    slope_cols = (8.0 * (right_one - left_one) - (right_two - left_two)) / 12.0
    spread = up_one + down_one + right_one + left_one - 4.0 * centre
    return (
        centre
        - courant[0] * slope_rows
        - courant[1] * slope_cols
        + diffusion[:, :, None, None] * spread
    )


HI = lax.Precision.HIGHEST
BLK = 8


def filter_kernel(obs_ref, err_ref, root_ref, raw_ref, wide_ref, out_ref, gram, shift, slope, inc, mean_ref, *, members, group):
    count = raw_ref.shape[0]
    lanes = gram.shape[1]
    freedom = members - 1.0
    raw = raw_ref[...]
    centre = jnp.sum(raw, axis=1, keepdims=True) / members
    anomaly = raw - centre
    mean_ref[...] = jnp.transpose(jnp.broadcast_to(centre, (count, 8 * 16)))[:8, :]
    gram[:, :count] = lax.dot_general(
        anomaly, anomaly * (1.0 / freedom), (((1,), (1,)), ((), ())), precision=HI,
        preferred_element_type=jnp.float32)
    gram[:, count:] = jnp.concatenate([anomaly * (1.0 / freedom), anomaly], axis=1)

    def lift(array, row, column):
        return jnp.broadcast_to(jnp.broadcast_to(array[:, column:column + 1], (BLK, 128))[row:row + 1, :], (BLK, 128))

    def block(position, first, last):
        base = pl.multiple_of(position * BLK, BLK)
        tile = pl.multiple_of((base // 128) * 128, 128)
        back = lax.rem(128 - lax.rem(base, 128), 128)
        panel = gram[pl.ds(base, BLK), :]
        weight = wide_ref[pl.ds(base, BLK), :]
        corner = pltpu.roll(gram[pl.ds(base, BLK), pl.ds(tile, 128)], back, 1)
        corner_w = pltpu.roll(wide_ref[pl.ds(base, BLK), pl.ds(tile, 128)], back, 1)
        corner_m = pltpu.roll(mean_ref[:, pl.ds(tile, 128)], back, 1)
        cell = {(k, l): lift(corner, l, k) for l in range(BLK) for k in range(l, BLK)}
        means = [jnp.broadcast_to(corner_m[:, k:k + 1], (BLK, 128)) for k in range(BLK)]
        rows = [[jnp.broadcast_to(panel[k:k + 1, c:c + 128], (BLK, 128)) for c in range(0, lanes, 128)] for k in range(BLK)]
        line = lax.broadcasted_iota(jnp.int32, (BLK, 128), 0)
        tiles = range(lanes // 128)
        keep_x = [jnp.zeros((BLK, 128), jnp.float32) for _ in tiles]
        keep_z = [jnp.zeros((BLK, 128), jnp.float32) for _ in tiles]
        keep_g = jnp.zeros((BLK, 128), jnp.float32)
        mean_row = [mean_ref[:, c:c + 128] for c in range(0, count, 128)]
        for i in range(BLK):
            err = err_ref[base + i]
            root = root_ref[base + i]
            v = cell[i, i]
            s = v + err
            t = lax.rsqrt(s)
            e = 1.0 / (s + root * (s * t))
            h = 0.5 * (e * v)
            d = (obs_ref[base + i] - means[i]) * (t * t)
            xs, zs = {}, {}
            for k in range(i + 1, BLK):
                q = cell[k, i]
                xs[k] = lift(corner_w, i, k) * q
                zs[k] = e * (q - h * xs[k])
                means[k] = means[k] + d * xs[k]
            for l in range(i + 1, BLK):
                for k in range(l, BLK):
                    cell[k, l] = cell[k, l] - xs[k] * zs[l] - zs[k] * xs[l]
            for c in range(lanes // 128):
                q = rows[i][c]
                x = jnp.broadcast_to(weight[i:i + 1, 128 * c:128 * c + 128], (BLK, 128)) * q
                z = e * (q - h * x)
                for k in range(i + 1, BLK):
                    rows[k][c] = rows[k][c] - xs[k] * z - zs[k] * x
                keep_x[c] = jnp.where(line == i, x, keep_x[c])
                keep_z[c] = jnp.where(line == i, z, keep_z[c])
                if c < count // 128:
                    mean_row[c] = mean_row[c] + d * x
                if c == lanes // 128 - 1:
                    keep_g = jnp.where(line == i, d - e * q, keep_g)
        for c in range(count // 128):
            mean_ref[:, 128 * c:128 * c + 128] = mean_row[c]
        x = jnp.concatenate(keep_x, axis=1)
        z = jnp.concatenate(keep_z, axis=1)
        shift[pl.ds(base, BLK), :] = x
        slope[pl.ds(base, BLK), :] = z
        inc[pl.ds(base, BLK), :] = keep_g
        left = jnp.concatenate([x[:, first:last], z[:, first:last]], axis=0)
        right = jnp.concatenate([z, x], axis=0)
        gram[first:last, :] = gram[first:last, :] - lax.dot_general(
            left, right, (((0,), (0,)), ((), ())), precision=HI, preferred_element_type=jnp.float32)

    for first in range(0, count, group):
        last = first + group

        def body(position, carry):
            block(position, first, last)
            return carry

        lax.fori_loop(first // BLK, last // BLK, body, 0)
        if last < count:
            x = shift[first:last, :]
            z = slope[first:last, :]
            left = jnp.concatenate([x[:, last:count], z[:, last:count]], axis=0)
            right = jnp.concatenate([z, x], axis=0)
            gram[last:count, :] = gram[last:count, :] - lax.dot_general(
                left, right, (((0,), (0,)), ((), ())), precision=HI, preferred_element_type=jnp.float32)
    whole = lax.dot_general(
        inc[...], shift[:, count:], (((0,), (0,)), ((), ())), precision=HI, preferred_element_type=jnp.float32)
    eye = (lax.broadcasted_iota(jnp.int32, (members, members), 0) == lax.broadcasted_iota(jnp.int32, (members, members), 1))
    out_ref[...] = whole[members:2 * members, :members] + eye.astype(jnp.float32)


def run_filter(raw, obs_value, obs_error, wide, group=64):
    count, members = raw.shape
    lanes = count + 2 * members
    smem = pl.BlockSpec(memory_space=pltpu.SMEM)
    vmem = pl.BlockSpec(memory_space=pltpu.VMEM)
    return pl.pallas_call(
        functools.partial(filter_kernel, members=members, group=group),
        out_shape=jax.ShapeDtypeStruct((members, members), jnp.float32),
        in_specs=[smem, smem, smem, vmem, vmem],
        out_specs=vmem,
        scratch_shapes=[
            pltpu.VMEM((count, lanes), jnp.float32),
            pltpu.VMEM((count, lanes), jnp.float32),
            pltpu.VMEM((count, lanes), jnp.float32),
            pltpu.VMEM((count, 128), jnp.float32),
            pltpu.VMEM((8, count), jnp.float32),
        ],
        compiler_params=pltpu.CompilerParams(vmem_limit_bytes=32 * 2**20),
    )(obs_value, obs_error, jnp.sqrt(obs_error), raw, wide)


def wide_weights(observation_row, localize, own, rows_here, members):
    owner = observation_row // rows_here
    tiles = localize.shape[0]
    hot = (owner[None, :] == jnp.arange(tiles, dtype=jnp.int32)[:, None]).astype(jnp.float32)
    across = lax.dot_general(localize, hot, (((0,), (0,)), ((), ())), precision=HI)
    count = owner.shape[0]
    return jnp.concatenate(
        [across, jnp.broadcast_to(own[:, None], (count, members)), jnp.zeros((count, members), jnp.float32)], axis=1)


def on_device(
    ensemble,
    courant,
    diffusion,
    observation_row,
    observation_column,
    observation_field,
    observation_level,
    obs_value,
    obs_error,
    localize,
):
    members_here = ensemble.shape[0]
    rows_here = ensemble.shape[3]
    state = ensemble
    for step_count in range(STEPS):
        extended = padded(state, (("tile", 3),), 2)
        state = advance(extended, courant, diffusion)
    tile_pos = lax.axis_index("tile")
    member_start = lax.axis_index("mem") * members_here
    ens_size = members_here * lax.axis_size("mem")
    obs_count = observation_row.shape[0]
    local_row = observation_row - tile_pos * rows_here
    owned = (local_row >= 0) & (local_row < rows_here)
    clipped = jnp.clip(local_row, 0, rows_here - 1)
    sampled = state[:, observation_field, observation_level, clipped, observation_column].T
    mine = jnp.where(owned[:, None], sampled, 0.0)
    placed = lax.dynamic_update_slice(
        jnp.zeros((obs_count, ens_size), jnp.float32), mine, (jnp.int32(0), member_start)
    )
    raw = lax.psum(placed, ("tile", "mem"))
    own = lax.dynamic_slice_in_dim(localize, tile_pos, 1, 0)[0]
    wide = wide_weights(observation_row, localize, own, rows_here, ens_size)
    turned = run_filter(raw, obs_value, obs_error, wide)
    flat_state = state.reshape(members_here, -1)
    my_rows = lax.dynamic_slice(turned, (member_start, jnp.int32(0)), (members_here, ens_size))
    result = jnp.dot(
        my_rows,
        lax.all_gather(flat_state, "mem", axis=0, tiled=True),
        precision=lax.Precision.HIGHEST,
    )
    return result.reshape(state.shape)


def solution(mesh):
    placed = (
        P("mem", None, None, "tile", None),
        P(None, None, "tile", None),
        P(),
        P(),
        P(),
        P(),
        P(),
        P(),
        P(),
        P(),
    )
    return jax.shard_map(
        on_device,
        mesh=mesh,
        in_specs=placed,
        out_specs=P("mem", None, None, "tile", None),
        check_vma=False,
    )
```

```python
import functools

import jax
import jax.numpy as jnp
from jax import lax
from jax.experimental import pallas as pl
from jax.experimental.pallas import tpu as pltpu
from jax.sharding import PartitionSpec as P

STEPS = 2
HI = lax.Precision.HIGHEST
BLK = 8
SUB = 8
GROUPS = ((0, 1), (2, 3))


def iota(shape, dim):
    return lax.broadcasted_iota(jnp.int32, shape, dim)


def step_kernel(cells_ref, below_ref, above_ref, courant_ref, spread_ref, *refs):
    out_ref = refs[-1]
    width = cells_ref.shape[-1]
    spread = spread_ref[0]
    for r in range(2):
        along, across = courant_ref[0, r], courant_ref[1, r]
        middle = 1.0 - 4.0 * spread
        up, down, two = spread - along * (2.0 / 3.0), spread + along * (2.0 / 3.0), along * (1.0 / 12.0)
        right, left, far = spread - across * (2.0 / 3.0), spread + across * (2.0 / 3.0), across * (1.0 / 12.0)
        for member in range(cells_ref.shape[0]):
            rows = [ref[member, 0, i] for ref in (below_ref, cells_ref, above_ref) for i in range(2)]
            centre = rows[2 + r]
            out_ref[member, 0, r] = (
                (middle * centre + two * (rows[4 + r] - rows[r]))
                + (up * rows[3 + r] + down * rows[1 + r])
                + (right * pltpu.roll(centre, width - 1, 1) + left * pltpu.roll(centre, 1, 1))
                + far * (pltpu.roll(centre, width - 2, 1) - pltpu.roll(centre, 2, 1))
            )


def forecast_step(cells, below, above, courant, spread, field, into=None):
    count, _, rows, levels, width = below.shape
    part = 8
    block = pl.BlockSpec((part, 1, rows, levels, width), lambda m: (m, 0, 0, 0, 0))
    fields, place, sofar = into or (1, 0, None)
    more = [] if sofar is None else [sofar]
    return pl.pallas_call(
        step_kernel,
        grid=(count // part,),
        out_shape=jax.ShapeDtypeStruct((count, fields, rows, levels, width), jnp.float32),
        in_specs=[
            block,
            block,
            block,
            pl.BlockSpec((2, rows, levels, width), lambda m: (0, 0, 0, 0)),
            pl.BlockSpec((1, levels, width), lambda m: (field, 0, 0)),
        ] + [pl.BlockSpec(memory_space=pl.ANY) for _ in more],
        out_specs=pl.BlockSpec((part, 1, rows, levels, width), lambda m: (m, place, 0, 0, 0)),
        input_output_aliases={5: 0} if more else {},
        cost_estimate=pl.CostEstimate(flops=26 * below.size, bytes_accessed=16 * below.size, transcendentals=0),
    )(cells, below, above, courant, spread, *more)


def sample_kernel(tile_ref, row_ref, column_ref, field_ref, level_ref, *refs):
    out_ref = refs[-1]
    fields = refs[:-1]
    members, count = out_ref.shape
    rows_here = fields[0].shape[2]
    first = tile_ref[0] * rows_here
    out_ref[...] = jnp.zeros(out_ref.shape, jnp.float32)
    line = iota((members, SUB, 128), 1)
    place = iota((members, 128), 1)

    def one(k, carry):
        row = row_ref[k] - first

        @pl.when((row >= 0) & (row < rows_here))
        def _():
            level = level_ref[k]
            column = column_ref[k]
            level_base = pl.multiple_of((level // SUB) * SUB, SUB)
            column_base = pl.multiple_of((column // 128) * 128, 128)
            target = pl.multiple_of((k // 128) * 128, 128)
            for f, (ref, inner) in enumerate((ref, g) for ref in fields for g in range(ref.shape[1])):

                @pl.when(field_ref[k] == f)
                def _(ref=ref, inner=inner):
                    seen = ref[:, inner, row, pl.ds(level_base, SUB), pl.ds(column_base, 128)]
                    value = jnp.sum(jnp.where(line == level - level_base, seen, 0.0), axis=1)
                    shift = lax.rem(k - column + 512, 128)
                    value = pltpu.roll(value, shift, 1)
                    kept = out_ref[:, pl.ds(target, 128)]
                    out_ref[:, pl.ds(target, 128)] = jnp.where(place == k - target, value, kept)

        return carry

    lax.fori_loop(0, count, one, 0)


def sample(state, tile_pos, row, column, field, level):
    smem = pl.BlockSpec(memory_space=pltpu.SMEM)
    vmem = pl.BlockSpec(memory_space=pltpu.VMEM)
    return pl.pallas_call(
        sample_kernel,
        out_shape=jax.ShapeDtypeStruct((state[0].shape[0], row.shape[0]), jnp.float32),
        in_specs=[smem] * 5 + [vmem] * len(state),
        out_specs=vmem,
        compiler_params=pltpu.CompilerParams(vmem_limit_bytes=32 * 2**20),
    )(tile_pos.reshape(1), row, column, field, level, *state)


def filter_kernel(obs_ref, err_ref, root_ref, raw_0, raw_1, raw_2, raw_3, wide_ref, high_ref, low_ref, gram, shift, slope, inc, mean_ref, *, members, group):
    count = raw_0.shape[1]
    lanes = gram.shape[1]
    freedom = members - 1.0
    here = raw_0.shape[0]
    raw = jnp.transpose(jnp.concatenate([raw_0[...], raw_1[...], raw_2[...], raw_3[...]], axis=0))
    centre = jnp.sum(raw, axis=1, keepdims=True) / members
    anomaly = raw - centre
    mean_ref[...] = jnp.transpose(jnp.broadcast_to(centre, (count, 8 * 16)))[:8, :]
    gram[:, :count] = lax.dot_general(
        anomaly, anomaly * (1.0 / freedom), (((1,), (1,)), ((), ())), precision=HI,
        preferred_element_type=jnp.float32)
    gram[:, count:] = jnp.concatenate([anomaly * (1.0 / freedom), anomaly], axis=1)

    def lift(array, row, column):
        return jnp.broadcast_to(jnp.broadcast_to(array[:, column:column + 1], (BLK, 128))[row:row + 1, :], (BLK, 128))

    def block(position, first, last):
        base = pl.multiple_of(position * BLK, BLK)
        tile = pl.multiple_of((base // 128) * 128, 128)
        back = lax.rem(128 - lax.rem(base, 128), 128)
        panel = gram[pl.ds(base, BLK), :]
        weight = wide_ref[pl.ds(base, BLK), :]
        corner = pltpu.roll(gram[pl.ds(base, BLK), pl.ds(tile, 128)], back, 1)
        corner_w = pltpu.roll(wide_ref[pl.ds(base, BLK), pl.ds(tile, 128)], back, 1)
        corner_m = pltpu.roll(mean_ref[:, pl.ds(tile, 128)], back, 1)
        cell = {(k, l): lift(corner, l, k) for l in range(BLK) for k in range(l, BLK)}
        means = [jnp.broadcast_to(corner_m[:, k:k + 1], (BLK, 128)) for k in range(BLK)]
        rows = [[jnp.broadcast_to(panel[k:k + 1, c:c + 128], (BLK, 128)) for c in range(0, lanes, 128)] for k in range(BLK)]
        line = lax.broadcasted_iota(jnp.int32, (BLK, 128), 0)
        tiles = range(lanes // 128)
        keep_x = [jnp.zeros((BLK, 128), jnp.float32) for _ in tiles]
        keep_z = [jnp.zeros((BLK, 128), jnp.float32) for _ in tiles]
        keep_g = jnp.zeros((BLK, 128), jnp.float32)
        mean_row = [mean_ref[:, c:c + 128] for c in range(0, count, 128)]
        for i in range(BLK):
            err = err_ref[base + i]
            root = root_ref[base + i]
            v = cell[i, i]
            s = v + err
            t = lax.rsqrt(s)
            e = 1.0 / (s + root * (s * t))
            h = 0.5 * (e * v)
            d = (obs_ref[base + i] - means[i]) * (t * t)
            xs, zs = {}, {}
            for k in range(i + 1, BLK):
                q = cell[k, i]
                xs[k] = lift(corner_w, i, k) * q
                zs[k] = e * (q - h * xs[k])
                means[k] = means[k] + d * xs[k]
            for l in range(i + 1, BLK):
                for k in range(l, BLK):
                    cell[k, l] = cell[k, l] - xs[k] * zs[l] - zs[k] * xs[l]
            for c in range(lanes // 128):
                q = rows[i][c]
                x = jnp.broadcast_to(weight[i:i + 1, 128 * c:128 * c + 128], (BLK, 128)) * q
                z = e * (q - h * x)
                for k in range(i + 1, BLK):
                    rows[k][c] = rows[k][c] - xs[k] * z - zs[k] * x
                keep_x[c] = jnp.where(line == i, x, keep_x[c])
                keep_z[c] = jnp.where(line == i, z, keep_z[c])
                if c < count // 128:
                    mean_row[c] = mean_row[c] + d * x
                if c == lanes // 128 - 1:
                    keep_g = jnp.where(line == i, d - e * q, keep_g)
        for c in range(count // 128):
            mean_ref[:, 128 * c:128 * c + 128] = mean_row[c]
        x = jnp.concatenate(keep_x, axis=1)
        z = jnp.concatenate(keep_z, axis=1)
        shift[pl.ds(base, BLK), :] = x
        slope[pl.ds(base, BLK), :] = z
        inc[pl.ds(base, BLK), :] = keep_g
        left = jnp.concatenate([x[:, first:last], z[:, first:last]], axis=0)
        right = jnp.concatenate([z, x], axis=0)
        gram[first:last, :] = gram[first:last, :] - lax.dot_general(
            left, right, (((0,), (0,)), ((), ())), precision=HI, preferred_element_type=jnp.float32)

    for first in range(0, count, group):
        last = first + group

        def body(position, carry):
            block(position, first, last)
            return carry

        lax.fori_loop(first // BLK, last // BLK, body, 0)
        if last < count:
            x = shift[first:last, :]
            z = slope[first:last, :]
            left = jnp.concatenate([x[:, last:count], z[:, last:count]], axis=0)
            right = jnp.concatenate([z, x], axis=0)
            gram[last:count, :] = gram[last:count, :] - lax.dot_general(
                left, right, (((0,), (0,)), ((), ())), precision=HI, preferred_element_type=jnp.float32)
    whole = lax.dot_general(
        inc[...], shift[:, count:], (((0,), (0,)), ((), ())), precision=HI, preferred_element_type=jnp.float32)
    mine = whole[members:members + here, :members]
    mine = mine + (iota(mine.shape, 0) == iota(mine.shape, 1)).astype(jnp.float32)
    tall, broad = high_ref.shape
    down = (iota((tall, here), 0) // SUB == iota((tall, here), 1)).astype(jnp.float32)
    over = (iota((members, broad), 1) // SUB == iota((members, broad), 0)).astype(jnp.float32)
    spread = jnp.dot(jnp.dot(down, mine, precision=HI), over, precision=HI)
    spread = jnp.where(iota((tall, broad), 0) % SUB == iota((tall, broad), 1) % SUB, spread, 0.0)
    high = spread.astype(jnp.bfloat16)
    high_ref[...] = high
    low_ref[...] = (spread - high.astype(jnp.float32)).astype(jnp.bfloat16)


def run_filter(pieces, obs_value, obs_error, wide, group=64):
    here, count = pieces[0].shape
    members = here * len(pieces)
    lanes = count + 2 * members
    smem = pl.BlockSpec(memory_space=pltpu.SMEM)
    vmem = pl.BlockSpec(memory_space=pltpu.VMEM)
    spread = jax.ShapeDtypeStruct((here * SUB, members * SUB), jnp.bfloat16)
    return pl.pallas_call(
        functools.partial(filter_kernel, members=members, group=group),
        out_shape=(spread, spread),
        in_specs=[smem] * 3 + [vmem] * 5,
        out_specs=(vmem, vmem),
        scratch_shapes=[
            pltpu.VMEM((count, lanes), jnp.float32),
            pltpu.VMEM((count, lanes), jnp.float32),
            pltpu.VMEM((count, lanes), jnp.float32),
            pltpu.VMEM((count, 128), jnp.float32),
            pltpu.VMEM((8, count), jnp.float32),
        ],
        compiler_params=pltpu.CompilerParams(vmem_limit_bytes=32 * 2**20),
    )(obs_value, obs_error, jnp.sqrt(obs_error), *pieces, wide)


def wide_weights(observation_row, localize, own, rows_here, members):
    owner = observation_row // rows_here
    tiles = localize.shape[0]
    hot = (owner[None, :] == jnp.arange(tiles, dtype=jnp.int32)[:, None]).astype(jnp.float32)
    across = lax.dot_general(localize, hot, (((0,), (0,)), ((), ())), precision=HI)
    count = owner.shape[0]
    return jnp.concatenate(
        [across, jnp.broadcast_to(own[:, None], (count, members)), jnp.zeros((count, members), jnp.float32)], axis=1)


def update_kernel(order_ref, high_ref, low_ref, *refs):
    out_ref = refs[-1]
    high = high_ref[...]
    low = low_ref[...]
    both = jnp.concatenate([high, low], axis=0)
    tall = high.shape[0]
    here = out_ref.shape[0]
    groups = refs[0].shape[0] // here
    for f, (ref, inner) in enumerate((ref, g) for ref in refs[:-1] for g in range(ref.shape[1])):
        for r in range(out_ref.shape[2]):
            cells = jnp.concatenate(
                [ref[pl.ds(order_ref[j] * here, here), inner, r].reshape(-1, ref.shape[-1]) for j in range(groups)], axis=0
            )
            top = cells.astype(jnp.bfloat16)
            rest = (cells - top.astype(jnp.float32)).astype(jnp.bfloat16)
            first = jnp.dot(both, top, preferred_element_type=jnp.float32)
            second = jnp.dot(high, rest, preferred_element_type=jnp.float32)
            total = first[:tall] + (first[tall:] + second)
            out_ref[:, f, r] = total.reshape(out_ref.shape[0], SUB, -1)


def update(order, high, low, gathered):
    flat = gathered
    _, _, rows, levels, width = flat[0].shape
    here = high.shape[0] // SUB
    fields = sum(p.shape[1] for p in flat)
    full = pl.BlockSpec(high.shape, lambda i: (0, 0))
    return pl.pallas_call(
        update_kernel,
        grid=(levels // SUB,),
        out_shape=jax.ShapeDtypeStruct((here, fields, rows, levels, width), jnp.float32),
        in_specs=[pl.BlockSpec(memory_space=pltpu.SMEM), full, full] + [pl.BlockSpec(p.shape[:2] + (rows, SUB, width), lambda i: (0, 0, 0, i, 0)) for p in flat],
        out_specs=pl.BlockSpec((here, fields, rows, SUB, width), lambda i: (0, 0, 0, i, 0)),
        compiler_params=pltpu.CompilerParams(vmem_limit_bytes=40 * 2**20),
    )(order, high, low, *flat)


def exchange(total, swaps):
    for pairs in swaps:
        total = total + lax.ppermute(total, "tile", pairs)
    return total


def on_device(
    ensemble,
    courant,
    diffusion,
    observation_row,
    observation_column,
    observation_field,
    observation_level,
    obs_value,
    obs_error,
    localize,
):
    members_here, fields, levels, rows_here, width = ensemble.shape
    tiles = lax.axis_size("tile")
    groups = lax.axis_size("mem")
    ens_size = members_here * groups
    tile_pos = lax.axis_index("tile")
    onward = [(i, (i + 1) % tiles) for i in range(tiles)]
    backward = [((i + 1) % tiles, i) for i in range(tiles)]
    start = jnp.transpose(ensemble, (0, 1, 3, 2, 4))
    flow = jnp.transpose(courant, (0, 2, 1, 3))
    spread = jnp.broadcast_to(diffusion[:, :, None], (fields, levels, width))
    own = lax.dynamic_slice_in_dim(localize, tile_pos, 1, 0)[0]
    wide = wide_weights(observation_row, localize, own, rows_here, ens_size)

    state = []
    for group in GROUPS:
        whole = None
        middle = []
        for f in group:
            cells = start[:, f:f + 1]
            below = lax.ppermute(cells, "tile", onward)
            above = lax.ppermute(cells, "tile", backward)
            middle.append(forecast_step(cells, below, above, flow, spread, f))
        for place, f in enumerate(group):
            below = lax.ppermute(middle[place], "tile", onward)
            above = lax.ppermute(middle[place], "tile", backward)
            whole = forecast_step(middle[place], below, above, flow, spread, f, (len(group), place, whole))
        state.append(whole)
    gathered = [lax.all_gather(cells, "mem", axis=0, tiled=True) for cells in state]
    seen = sample(state, tile_pos, observation_row, observation_column, observation_field, observation_level)
    swaps = [[(i, i ^ bit) for i in range(tiles)] for bit in (1, 2, 4, 8, 16, 32)]
    seen = exchange(seen, swaps)
    pieces = [seen] + [lax.ppermute(seen, "mem", [(i, (i + d) % groups) for i in range(groups)]) for d in range(1, groups)]
    high, low = run_filter(pieces, obs_value, obs_error, wide)
    order = lax.rem(lax.axis_index("mem") - jnp.arange(groups, dtype=jnp.int32) + groups, groups)
    result = update(order, high, low, gathered)
    return jnp.transpose(result, (0, 1, 3, 2, 4))


def solution(mesh):
    placed = (
        P("mem", None, None, "tile", None),
        P(None, None, "tile", None),
        P(),
        P(),
        P(),
        P(),
        P(),
        P(),
        P(),
        P(),
    )
    return jax.shard_map(
        on_device,
        mesh=mesh,
        in_specs=placed,
        out_specs=P("mem", None, None, "tile", None),
        check_vma=False,
    )
```

```python
import functools

import jax
import jax.numpy as jnp
from jax import lax
from jax.experimental import pallas as pl
from jax.experimental.pallas import tpu as pltpu
from jax.sharding import PartitionSpec as P

STEPS = 2
HI = lax.Precision.HIGHEST
BLK = 8
SUB = 8
GROUPS = ((0, 1), (2, 3))


def iota(shape, dim):
    return lax.broadcasted_iota(jnp.int32, shape, dim)


def step_kernel(split, cells_ref, below_ref, above_ref, courant_ref, spread_ref, *refs):
    out_ref = refs[-1]
    width = cells_ref.shape[-1]
    spread = spread_ref[0]
    for r in range(2):
        along, across = courant_ref[0, r], courant_ref[1, r]
        middle = 1.0 - 4.0 * spread
        up, down, two = spread - along * (2.0 / 3.0), spread + along * (2.0 / 3.0), along * (1.0 / 12.0)
        right, left, far = spread - across * (2.0 / 3.0), spread + across * (2.0 / 3.0), across * (1.0 / 12.0)
        for member in range(cells_ref.shape[0]):
            rows = [ref[member, 0, i] for ref in (below_ref, cells_ref, above_ref) for i in range(2)]
            centre = rows[2 + r]
            value = (
                (middle * centre + two * (rows[4 + r] - rows[r]))
                + (up * rows[3 + r] + down * rows[1 + r])
                + (right * pltpu.roll(centre, width - 1, 1) + left * pltpu.roll(centre, 1, 1))
                + far * (pltpu.roll(centre, width - 2, 1) - pltpu.roll(centre, 2, 1))
            )
            if split:
                for half in range(2):
                    out_ref[2 * r + half, member, 0] = value[:, half * (width // 2):(half + 1) * (width // 2)]
            else:
                out_ref[member, 0, r] = value


def forecast_step(cells, below, above, courant, spread, field, into=None, split=False):
    count, _, rows, levels, width = below.shape
    part = 8
    block = pl.BlockSpec((part, 1, rows, levels, width), lambda m: (m, 0, 0, 0, 0))
    fields, place, sofar = into or (1, 0, None)
    more = [] if sofar is None else [sofar]
    if split:
        shape = (2 * rows, count, fields, levels, width // 2)
        out_block = pl.BlockSpec((2 * rows, part, 1, levels, width // 2), lambda m: (0, m, place, 0, 0))
    else:
        shape = (count, fields, rows, levels, width)
        out_block = pl.BlockSpec((part, 1, rows, levels, width), lambda m: (m, place, 0, 0, 0))
    return pl.pallas_call(
        functools.partial(step_kernel, split),
        grid=(count // part,),
        out_shape=jax.ShapeDtypeStruct(shape, jnp.float32),
        in_specs=[
            block,
            block,
            block,
            pl.BlockSpec((2, rows, levels, width), lambda m: (0, 0, 0, 0)),
            pl.BlockSpec((1, levels, width), lambda m: (field, 0, 0)),
        ] + [pl.BlockSpec(memory_space=pl.ANY) for _ in more],
        out_specs=out_block,
        input_output_aliases={5: 0} if more else {},
        cost_estimate=pl.CostEstimate(flops=below.size, bytes_accessed=below.size, transcendentals=0),
    )(cells, below, above, courant, spread, *more)


def sample_kernel(tile_ref, row_ref, column_ref, field_ref, level_ref, whole_ref, split_ref, out_ref, mine):
    members, count = out_ref.shape
    early, rows_here = whole_ref.shape[1:3]
    first = tile_ref[0] * rows_here
    out_ref[...] = jnp.zeros(out_ref.shape, jnp.float32)
    line = iota((members, SUB, 128), 1)
    place = iota((members, 128), 1)

    def look(k, found):
        mine[found] = k
        row = row_ref[k] - first
        return found + ((row >= 0) & (row < rows_here)).astype(jnp.int32)

    found = lax.fori_loop(0, count, look, jnp.int32(0), unroll=8)

    def one(index, carry):
        k = mine[index]
        row = row_ref[k] - first
        level = level_ref[k]
        column = column_ref[k]
        field = field_ref[k]
        level_base = pl.multiple_of((level // SUB) * SUB, SUB)
        column_base = pl.multiple_of((column // 128) * 128, 128)
        target = pl.multiple_of((k // 128) * 128, 128)

        def put(seen):
            value = jnp.sum(jnp.where(line == level - level_base, seen, 0.0), axis=1)
            value = pltpu.roll(value, lax.rem(k - column + 512, 128), 1)
            kept = out_ref[:, pl.ds(target, 128)]
            out_ref[:, pl.ds(target, 128)] = jnp.where(place == k - target, value, kept)

        @pl.when(field < early)
        def _():
            put(whole_ref[:, field, row, pl.ds(level_base, SUB), pl.ds(column_base, 128)])

        @pl.when(field >= early)
        def _():
            put(split_ref[2 * row + column // 128, :, field - early, pl.ds(level_base, SUB), :])

        return carry

    lax.fori_loop(0, found, one, 0)


def sample(whole, split, tile_pos, row, column, field, level):
    smem = pl.BlockSpec(memory_space=pltpu.SMEM)
    vmem = pl.BlockSpec(memory_space=pltpu.VMEM)
    return pl.pallas_call(
        sample_kernel,
        out_shape=jax.ShapeDtypeStruct((whole.shape[0], row.shape[0]), jnp.float32),
        in_specs=[smem] * 5 + [vmem] * 2,
        out_specs=vmem,
        scratch_shapes=[pltpu.SMEM((row.shape[0] + 1,), jnp.int32)],
        compiler_params=pltpu.CompilerParams(vmem_limit_bytes=32 * 2**20),
    )(tile_pos.reshape(1), row, column, field, level, whole, split)


def filter_kernel(order_ref, obs_ref, err_ref, root_ref, raw_0, raw_1, raw_2, raw_3, wide_ref, high_ref, low_ref, joined, gram, shift, slope, inc, mean_ref, *, members, group):
    count = raw_0.shape[1]
    lanes = gram.shape[1]
    freedom = members - 1.0
    here = raw_0.shape[0]
    for j, piece in enumerate((raw_0, raw_1, raw_2, raw_3)):
        joined[pl.ds(pl.multiple_of(order_ref[j] * here, here), here), :] = piece[...]
    raw = jnp.transpose(joined[...])
    centre = jnp.sum(raw, axis=1, keepdims=True) / members
    anomaly = raw - centre
    mean_ref[...] = jnp.transpose(jnp.broadcast_to(centre, (count, 8 * 16)))[:8, :]
    gram[:, :count] = lax.dot_general(
        anomaly, anomaly * (1.0 / freedom), (((1,), (1,)), ((), ())), precision=HI,
        preferred_element_type=jnp.float32)
    gram[:, count:] = jnp.concatenate([anomaly * (1.0 / freedom), anomaly], axis=1)

    def lift(array, row, column):
        return jnp.broadcast_to(jnp.broadcast_to(array[:, column:column + 1], (BLK, 128))[row:row + 1, :], (BLK, 128))

    def block(position, first, last):
        base = pl.multiple_of(position * BLK, BLK)
        tile = pl.multiple_of((base // 128) * 128, 128)
        back = lax.rem(128 - lax.rem(base, 128), 128)
        panel = gram[pl.ds(base, BLK), :]
        weight = wide_ref[pl.ds(base, BLK), :]
        corner = pltpu.roll(gram[pl.ds(base, BLK), pl.ds(tile, 128)], back, 1)
        corner_w = pltpu.roll(wide_ref[pl.ds(base, BLK), pl.ds(tile, 128)], back, 1)
        corner_m = pltpu.roll(mean_ref[:, pl.ds(tile, 128)], back, 1)
        cell = {(k, l): lift(corner, l, k) for l in range(BLK) for k in range(l, BLK)}
        means = [jnp.broadcast_to(corner_m[:, k:k + 1], (BLK, 128)) for k in range(BLK)]
        rows = [[jnp.broadcast_to(panel[k:k + 1, c:c + 128], (BLK, 128)) for c in range(0, lanes, 128)] for k in range(BLK)]
        line = lax.broadcasted_iota(jnp.int32, (BLK, 128), 0)
        tiles = range(lanes // 128)
        keep_x = [jnp.zeros((BLK, 128), jnp.float32) for _ in tiles]
        keep_z = [jnp.zeros((BLK, 128), jnp.float32) for _ in tiles]
        keep_g = jnp.zeros((BLK, 128), jnp.float32)
        mean_row = [mean_ref[:, c:c + 128] for c in range(0, count, 128)]
        for i in range(BLK):
            err = err_ref[base + i]
            root = root_ref[base + i]
            v = cell[i, i]
            s = v + err
            t = lax.rsqrt(s)
            e = 1.0 / (s + root * (s * t))
            h = 0.5 * (e * v)
            d = (obs_ref[base + i] - means[i]) * (t * t)
            xs, zs = {}, {}
            for k in range(i + 1, BLK):
                q = cell[k, i]
                xs[k] = lift(corner_w, i, k) * q
                zs[k] = e * (q - h * xs[k])
                means[k] = means[k] + d * xs[k]
            for l in range(i + 1, BLK):
                for k in range(l, BLK):
                    cell[k, l] = cell[k, l] - xs[k] * zs[l] - zs[k] * xs[l]
            for c in range(lanes // 128):
                q = rows[i][c]
                x = jnp.broadcast_to(weight[i:i + 1, 128 * c:128 * c + 128], (BLK, 128)) * q
                z = e * (q - h * x)
                for k in range(i + 1, BLK):
                    rows[k][c] = rows[k][c] - xs[k] * z - zs[k] * x
                keep_x[c] = jnp.where(line == i, x, keep_x[c])
                keep_z[c] = jnp.where(line == i, z, keep_z[c])
                if c < count // 128:
                    mean_row[c] = mean_row[c] + d * x
                if c == lanes // 128 - 1:
                    keep_g = jnp.where(line == i, d - e * q, keep_g)
        for c in range(count // 128):
            mean_ref[:, 128 * c:128 * c + 128] = mean_row[c]
        x = jnp.concatenate(keep_x, axis=1)
        z = jnp.concatenate(keep_z, axis=1)
        shift[pl.ds(base, BLK), :] = x
        slope[pl.ds(base, BLK), :] = z
        inc[pl.ds(base, BLK), :] = keep_g
        left = jnp.concatenate([x[:, first:last], z[:, first:last]], axis=0)
        right = jnp.concatenate([z, x], axis=0)
        gram[first:last, :] = gram[first:last, :] - lax.dot_general(
            left, right, (((0,), (0,)), ((), ())), precision=HI, preferred_element_type=jnp.float32)

    for first in range(0, count, group):
        last = first + group

        def body(position, carry):
            block(position, first, last)
            return carry

        lax.fori_loop(first // BLK, last // BLK, body, 0)
        if last < count:
            x = shift[first:last, :]
            z = slope[first:last, :]
            left = jnp.concatenate([x[:, last:count], z[:, last:count]], axis=0)
            right = jnp.concatenate([z, x], axis=0)
            gram[last:count, :] = gram[last:count, :] - lax.dot_general(
                left, right, (((0,), (0,)), ((), ())), precision=HI, preferred_element_type=jnp.float32)
    whole = lax.dot_general(
        inc[...], shift[:, count:], (((0,), (0,)), ((), ())), precision=HI, preferred_element_type=jnp.float32)
    mine = whole[members:2 * members, :members]
    mine = mine + (iota(mine.shape, 0) == iota(mine.shape, 1)).astype(jnp.float32)
    tall, broad = high_ref.shape
    down = (iota((tall, members), 0) // SUB == iota((tall, members), 1)).astype(jnp.float32)
    over = (iota((members, broad), 1) // SUB == iota((members, broad), 0)).astype(jnp.float32)
    spread = jnp.dot(jnp.dot(down, mine, precision=HI), over, precision=HI)
    spread = jnp.where(iota((tall, broad), 0) % SUB == iota((tall, broad), 1) % SUB, spread, 0.0)
    high = spread.astype(jnp.bfloat16)
    high_ref[...] = high
    low_ref[...] = (spread - high.astype(jnp.float32)).astype(jnp.bfloat16)


def run_filter(order, pieces, obs_value, obs_error, wide, group=64):
    here, count = pieces[0].shape
    members = here * len(pieces)
    lanes = count + 2 * members
    smem = pl.BlockSpec(memory_space=pltpu.SMEM)
    vmem = pl.BlockSpec(memory_space=pltpu.VMEM)
    spread = jax.ShapeDtypeStruct((members * SUB, members * SUB), jnp.bfloat16)
    return pl.pallas_call(
        functools.partial(filter_kernel, members=members, group=group),
        out_shape=(spread, spread),
        in_specs=[smem] * 4 + [vmem] * 5,
        out_specs=(vmem, vmem),
        scratch_shapes=[
            pltpu.VMEM((members, count), jnp.float32),
            pltpu.VMEM((count, lanes), jnp.float32),
            pltpu.VMEM((count, lanes), jnp.float32),
            pltpu.VMEM((count, lanes), jnp.float32),
            pltpu.VMEM((count, 128), jnp.float32),
            pltpu.VMEM((8, count), jnp.float32),
        ],
        compiler_params=pltpu.CompilerParams(vmem_limit_bytes=32 * 2**20),
    )(order, obs_value, obs_error, jnp.sqrt(obs_error), *pieces, wide)


def wide_weights(observation_row, localize, own, rows_here, members):
    owner = observation_row // rows_here
    tiles = localize.shape[0]
    hot = (owner[None, :] == jnp.arange(tiles, dtype=jnp.int32)[:, None]).astype(jnp.float32)
    across = lax.dot_general(localize, hot, (((0,), (0,)), ((), ())), precision=HI)
    count = owner.shape[0]
    return jnp.concatenate(
        [across, jnp.broadcast_to(own[:, None], (count, members)), jnp.zeros((count, members), jnp.float32)], axis=1)


def product(high, low, cells):
    both = jnp.concatenate([high, low], axis=0)
    tall = high.shape[0]
    top = cells.astype(jnp.bfloat16)
    rest = (cells - top.astype(jnp.float32)).astype(jnp.bfloat16)
    first = jnp.dot(both, top, preferred_element_type=jnp.float32)
    second = jnp.dot(high, rest, preferred_element_type=jnp.float32)
    return first[:tall] + (first[tall:] + second)


def gathered_kernel(mem_ref, high_ref, low_ref, cells_ref, out_ref):
    here = out_ref.shape[0]
    mine = pl.ds(pl.multiple_of(mem_ref[0] * here * SUB, here * SUB), here * SUB)
    high, low = high_ref[mine, :], low_ref[mine, :]
    for f in range(out_ref.shape[1]):
        for r in range(out_ref.shape[2]):
            cells = cells_ref[:, f, r].reshape(-1, cells_ref.shape[-1])
            out_ref[:, f, r] = product(high, low, cells).reshape(here, SUB, -1)


def update_gathered(mem_pos, high, low, cells, all_fields):
    members, fields, rows, levels, width = cells.shape
    here = members // 4
    full = pl.BlockSpec(high.shape, lambda i: (0, 0))
    return pl.pallas_call(
        gathered_kernel,
        grid=(levels // SUB,),
        out_shape=jax.ShapeDtypeStruct((here, all_fields, rows, levels, width), jnp.float32),
        in_specs=[
            pl.BlockSpec(memory_space=pltpu.SMEM), full, full,
            pl.BlockSpec((members, fields, rows, SUB, width), lambda i: (0, 0, 0, i, 0)),
        ],
        out_specs=pl.BlockSpec((here, fields, rows, SUB, width), lambda i: (0, 0, 0, i, 0)),
        compiler_params=pltpu.CompilerParams(vmem_limit_bytes=40 * 2**20),
    )(mem_pos.reshape(1), high, low, cells)


def piece_kernel(high_ref, low_ref, cells_ref, out_ref):
    groups, here, fields, _, width = cells_ref.shape
    cells = jnp.concatenate([cells_ref[:, :, f].reshape(-1, width) for f in range(fields)], axis=1)
    total = product(high_ref[...], low_ref[...], cells)
    for f in range(fields):
        out_ref[:, :, f] = total[:, f * width:(f + 1) * width].reshape(groups, here, SUB, width)


def update_piece(high, low, cells):
    groups, here, fields, levels, width = cells.shape
    full = pl.BlockSpec(high.shape, lambda i: (0, 0))
    block = pl.BlockSpec((groups, here, fields, SUB, width), lambda i: (0, 0, 0, i, 0))
    return pl.pallas_call(
        piece_kernel,
        grid=(levels // SUB,),
        out_shape=jax.ShapeDtypeStruct(cells.shape, jnp.float32),
        in_specs=[full, full, block],
        out_specs=block,
        compiler_params=pltpu.CompilerParams(vmem_limit_bytes=40 * 2**20),
    )(high, low, cells)


def join_kernel(back_ref, sofar_ref, out_ref):
    half = back_ref.shape[-1]
    for piece in range(back_ref.shape[0]):
        r, h = piece // 2, piece % 2
        out_ref[:, :, r, :, h * half:(h + 1) * half] = back_ref[piece]


def join(back, sofar):
    pieces, here, fields, levels, half = back.shape
    part = 8
    place = sofar.shape[1] // fields - 1
    return pl.pallas_call(
        join_kernel,
        grid=(here // part,),
        out_shape=jax.ShapeDtypeStruct(sofar.shape, jnp.float32),
        in_specs=[
            pl.BlockSpec((pieces, part, fields, levels, half), lambda m: (0, m, 0, 0, 0)),
            pl.BlockSpec(memory_space=pl.ANY),
        ],
        out_specs=pl.BlockSpec((part, fields) + sofar.shape[2:], lambda m: (m, place, 0, 0, 0)),
        input_output_aliases={1: 0},
    )(back, sofar)


def after(value, *others):
    return lax.optimization_barrier((value,) + others)[0]


def on_device(
    ensemble,
    courant,
    diffusion,
    observation_row,
    observation_column,
    observation_field,
    observation_level,
    obs_value,
    obs_error,
    localize,
):
    members_here, fields, levels, rows_here, width = ensemble.shape
    tiles = lax.axis_size("tile")
    groups = lax.axis_size("mem")
    ens_size = members_here * groups
    tile_pos = lax.axis_index("tile")
    onward = [(i, (i + 1) % tiles) for i in range(tiles)]
    backward = [((i + 1) % tiles, i) for i in range(tiles)]
    start = jnp.transpose(ensemble, (0, 1, 3, 2, 4))
    flow = jnp.transpose(courant, (0, 2, 1, 3))
    spread = jnp.broadcast_to(diffusion[:, :, None], (fields, levels, width))
    own = lax.dynamic_slice_in_dim(localize, tile_pos, 1, 0)[0]
    wide = wide_weights(observation_row, localize, own, rows_here, ens_size)

    mem_pos = lax.axis_index("mem")
    order = lax.rem(mem_pos - jnp.arange(groups, dtype=jnp.int32) + groups, groups)

    def shifted(array, by):
        return lax.ppermute(array, "tile", [(i, (i + by) % tiles) for i in range(tiles)])

    def step(cells, f, into=None, split=False, wait=()):
        below, above = shifted(cells, 1), shifted(cells, -1)
        if wait:
            below = after(below, *wait)
        return forecast_step(cells, below, above, flow, spread, f, into, split)

    middle = [step(start[:, f:f + 1], f) for f in range(fields)]

    def last_step(fields_of, split, wait):
        whole = None
        for place, f in enumerate(fields_of):
            whole = step(middle[f], f, (len(fields_of), place, whole), split, wait)
        return whole

    whole = last_step(GROUPS[0], False, middle)
    split = last_step(GROUPS[1], True, (whole,))
    gathered = lax.all_gather(after(whole, split), "mem", axis=0, tiled=True)
    swapped = lax.all_to_all(split, "mem", 0, 0, tiled=True)
    seen = sample(
        whole, split, tile_pos, observation_row, observation_column, observation_field, observation_level
    )
    for bit in (1, 2, 4, 8, 16, 32):
        seen = seen + lax.ppermute(seen, "tile", [(i, i ^ bit) for i in range(tiles)])
    pieces = [seen] + [lax.ppermute(seen, "mem", [(i, (i + d) % groups) for i in range(groups)]) for d in range(1, groups)]
    high, low = run_filter(order, pieces, obs_value, obs_error, wide)
    back = lax.all_to_all(update_piece(high, low, swapped), "mem", 0, 0, tiled=True)
    result = update_gathered(mem_pos, high, low, gathered, fields)
    return jnp.transpose(join(back, result), (0, 1, 3, 2, 4))


def solution(mesh):
    placed = (
        P("mem", None, None, "tile", None),
        P(None, None, "tile", None),
        P(),
        P(),
        P(),
        P(),
        P(),
        P(),
        P(),
        P(),
    )
    return jax.shard_map(
        on_device,
        mesh=mesh,
        in_specs=placed,
        out_specs=P("mem", None, None, "tile", None),
        check_vma=False,
    )
```

```python
import functools

import jax
import jax.numpy as jnp
from jax import lax
from jax.experimental import pallas as pl
from jax.experimental.pallas import tpu as pltpu
from jax.sharding import PartitionSpec as P

STEPS = 2
HI = lax.Precision.HIGHEST
BLK = 8
SUB = 8
GROUPS = ((0, 1), (2, 3))


def iota(shape, dim):
    return lax.broadcasted_iota(jnp.int32, shape, dim)


def step_kernel(split, cells_ref, below_ref, above_ref, courant_ref, spread_ref, *refs):
    out_ref = refs[-1]
    width = cells_ref.shape[-1]
    spread = spread_ref[0]
    for r in range(2):
        along, across = courant_ref[0, r], courant_ref[1, r]
        middle = 1.0 - 4.0 * spread
        up, down, two = spread - along * (2.0 / 3.0), spread + along * (2.0 / 3.0), along * (1.0 / 12.0)
        right, left, far = spread - across * (2.0 / 3.0), spread + across * (2.0 / 3.0), across * (1.0 / 12.0)
        for member in range(cells_ref.shape[0]):
            rows = [ref[member, 0, i] for ref in (below_ref, cells_ref, above_ref) for i in range(2)]
            centre = rows[2 + r]
            value = (
                (middle * centre + two * (rows[4 + r] - rows[r]))
                + (up * rows[3 + r] + down * rows[1 + r])
                + (right * pltpu.roll(centre, width - 1, 1) + left * pltpu.roll(centre, 1, 1))
                + far * (pltpu.roll(centre, width - 2, 1) - pltpu.roll(centre, 2, 1))
            )
            if split:
                for half in range(2):
                    out_ref[2 * r + half, member, 0] = value[:, half * (width // 2):(half + 1) * (width // 2)]
            else:
                out_ref[member, 0, r] = value


def forecast_step(cells, below, above, courant, spread, field, into=None, split=False):
    count, _, rows, levels, width = below.shape
    part = 8
    block = pl.BlockSpec((part, 1, rows, levels, width), lambda m: (m, 0, 0, 0, 0))
    fields, place, sofar = into or (1, 0, None)
    more = [] if sofar is None else [sofar]
    if split:
        shape = (2 * rows, count, fields, levels, width // 2)
        out_block = pl.BlockSpec((2 * rows, part, 1, levels, width // 2), lambda m: (0, m, place, 0, 0))
    else:
        shape = (count, fields, rows, levels, width)
        out_block = pl.BlockSpec((part, 1, rows, levels, width), lambda m: (m, place, 0, 0, 0))
    return pl.pallas_call(
        functools.partial(step_kernel, split),
        grid=(count // part,),
        out_shape=jax.ShapeDtypeStruct(shape, jnp.float32),
        in_specs=[
            block,
            block,
            block,
            pl.BlockSpec((2, rows, levels, width), lambda m: (0, 0, 0, 0)),
            pl.BlockSpec((1, levels, width), lambda m: (field, 0, 0)),
        ] + [pl.BlockSpec(memory_space=pl.ANY) for _ in more],
        out_specs=out_block,
        input_output_aliases={5: 0} if more else {},
        cost_estimate=pl.CostEstimate(flops=below.size, bytes_accessed=below.size, transcendentals=0),
    )(cells, below, above, courant, spread, *more)


def sample_kernel(tile_ref, row_ref, column_ref, field_ref, level_ref, whole_ref, split_ref, out_ref, mine):
    members, count = out_ref.shape
    early, rows_here = whole_ref.shape[1:3]
    first = tile_ref[0] * rows_here
    out_ref[...] = jnp.zeros(out_ref.shape, jnp.float32)
    line = iota((members, SUB, 128), 1)
    place = iota((members, 128), 1)

    def look(k, found):
        mine[found] = k
        row = row_ref[k] - first
        return found + ((row >= 0) & (row < rows_here)).astype(jnp.int32)

    found = lax.fori_loop(0, count, look, jnp.int32(0), unroll=8)

    def one(index, carry):
        k = mine[index]
        row = row_ref[k] - first
        level = level_ref[k]
        column = column_ref[k]
        field = field_ref[k]
        level_base = pl.multiple_of((level // SUB) * SUB, SUB)
        column_base = pl.multiple_of((column // 128) * 128, 128)
        target = pl.multiple_of((k // 128) * 128, 128)

        def put(seen):
            value = jnp.sum(jnp.where(line == level - level_base, seen, 0.0), axis=1)
            value = pltpu.roll(value, lax.rem(k - column + 512, 128), 1)
            kept = out_ref[:, pl.ds(target, 128)]
            out_ref[:, pl.ds(target, 128)] = jnp.where(place == k - target, value, kept)

        @pl.when(field < early)
        def _():
            put(whole_ref[:, field, row, pl.ds(level_base, SUB), pl.ds(column_base, 128)])

        @pl.when(field >= early)
        def _():
            put(split_ref[2 * row + column // 128, :, field - early, pl.ds(level_base, SUB), :])

        return carry

    lax.fori_loop(0, found, one, 0)


def sample(whole, split, tile_pos, row, column, field, level):
    smem = pl.BlockSpec(memory_space=pltpu.SMEM)
    vmem = pl.BlockSpec(memory_space=pltpu.VMEM)
    return pl.pallas_call(
        sample_kernel,
        out_shape=jax.ShapeDtypeStruct((whole.shape[0], row.shape[0]), jnp.float32),
        in_specs=[smem] * 5 + [vmem] * 2,
        out_specs=vmem,
        scratch_shapes=[pltpu.SMEM((row.shape[0] + 1,), jnp.int32)],
        compiler_params=pltpu.CompilerParams(vmem_limit_bytes=32 * 2**20),
    )(tile_pos.reshape(1), row, column, field, level, whole, split)


def filter_kernel(order_ref, obs_ref, err_ref, root_ref, raw_0, raw_1, raw_2, raw_3, wide_ref, high_ref, low_ref, joined, gram, shift, slope, inc, mean_ref, *, members, group):
    count = raw_0.shape[1]
    lanes = gram.shape[1]
    freedom = members - 1.0
    here = raw_0.shape[0]
    for j, piece in enumerate((raw_0, raw_1, raw_2, raw_3)):
        joined[pl.ds(pl.multiple_of(order_ref[j] * here, here), here), :] = piece[...]
    raw = jnp.transpose(joined[...])
    centre = jnp.sum(raw, axis=1, keepdims=True) / members
    anomaly = raw - centre
    mean_ref[...] = jnp.transpose(jnp.broadcast_to(centre, (count, 8 * 16)))[:8, :]
    gram[:, :count] = lax.dot_general(
        anomaly, anomaly * (1.0 / freedom), (((1,), (1,)), ((), ())), precision=HI,
        preferred_element_type=jnp.float32)
    gram[:, count:] = jnp.concatenate([anomaly * (1.0 / freedom), anomaly], axis=1)

    def lift(array, row, column):
        return jnp.broadcast_to(jnp.broadcast_to(array[:, column:column + 1], (BLK, 128))[row:row + 1, :], (BLK, 128))

    def block(position, first, last):
        base = pl.multiple_of(position * BLK, BLK)
        tile = pl.multiple_of((base // 128) * 128, 128)
        back = lax.rem(128 - lax.rem(base, 128), 128)
        panel = gram[pl.ds(base, BLK), :]
        weight = wide_ref[pl.ds(base, BLK), :]
        corner = pltpu.roll(gram[pl.ds(base, BLK), pl.ds(tile, 128)], back, 1)
        corner_w = pltpu.roll(wide_ref[pl.ds(base, BLK), pl.ds(tile, 128)], back, 1)
        corner_m = pltpu.roll(mean_ref[:, pl.ds(tile, 128)], back, 1)
        cell = {(k, l): lift(corner, l, k) for l in range(BLK) for k in range(l, BLK)}
        means = [jnp.broadcast_to(corner_m[:, k:k + 1], (BLK, 128)) for k in range(BLK)]
        rows = [[jnp.broadcast_to(panel[k:k + 1, c:c + 128], (BLK, 128)) for c in range(0, lanes, 128)] for k in range(BLK)]
        line = lax.broadcasted_iota(jnp.int32, (BLK, 128), 0)
        tiles = range(lanes // 128)
        keep_x = [jnp.zeros((BLK, 128), jnp.float32) for _ in tiles]
        keep_z = [jnp.zeros((BLK, 128), jnp.float32) for _ in tiles]
        keep_g = jnp.zeros((BLK, 128), jnp.float32)
        mean_row = [mean_ref[:, c:c + 128] for c in range(0, count, 128)]
        for i in range(BLK):
            err = err_ref[base + i]
            root = root_ref[base + i]
            v = cell[i, i]
            s = v + err
            t = lax.rsqrt(s)
            e = 1.0 / (s + root * (s * t))
            h = 0.5 * (e * v)
            d = (obs_ref[base + i] - means[i]) * (t * t)
            xs, zs = {}, {}
            for k in range(i + 1, BLK):
                q = cell[k, i]
                xs[k] = lift(corner_w, i, k) * q
                zs[k] = e * (q - h * xs[k])
                means[k] = means[k] + d * xs[k]
            for l in range(i + 1, BLK):
                for k in range(l, BLK):
                    cell[k, l] = cell[k, l] - xs[k] * zs[l] - zs[k] * xs[l]
            for c in range(lanes // 128):
                q = rows[i][c]
                x = jnp.broadcast_to(weight[i:i + 1, 128 * c:128 * c + 128], (BLK, 128)) * q
                z = e * (q - h * x)
                for k in range(i + 1, BLK):
                    rows[k][c] = rows[k][c] - xs[k] * z - zs[k] * x
                keep_x[c] = jnp.where(line == i, x, keep_x[c])
                keep_z[c] = jnp.where(line == i, z, keep_z[c])
                if c < count // 128:
                    mean_row[c] = mean_row[c] + d * x
                if c == lanes // 128 - 1:
                    keep_g = jnp.where(line == i, d - e * q, keep_g)
        for c in range(count // 128):
            mean_ref[:, 128 * c:128 * c + 128] = mean_row[c]
        x = jnp.concatenate(keep_x, axis=1)
        z = jnp.concatenate(keep_z, axis=1)
        shift[pl.ds(base, BLK), :] = x
        slope[pl.ds(base, BLK), :] = z
        inc[pl.ds(base, BLK), :] = keep_g
        left = jnp.concatenate([x[:, first:last], z[:, first:last]], axis=0)
        right = jnp.concatenate([z, x], axis=0)
        left_top, right_top = left.astype(jnp.bfloat16), right.astype(jnp.bfloat16)
        left_rest = (left - left_top.astype(jnp.float32)).astype(jnp.bfloat16)
        right_rest = (right - right_top.astype(jnp.float32)).astype(jnp.bfloat16)
        gram[first:last, :] = gram[first:last, :] - lax.dot_general(
            jnp.concatenate([left_top, left_rest, left_top], axis=0),
            jnp.concatenate([right_top, right_top, right_rest], axis=0),
            (((0,), (0,)), ((), ())), preferred_element_type=jnp.float32)

    for first in range(0, count, group):
        last = first + group

        def body(position, carry):
            block(position, first, last)
            return carry

        lax.fori_loop(first // BLK, last // BLK, body, 0)
        if last < count:
            x = shift[first:last, :]
            z = slope[first:last, :]
            left = jnp.concatenate([x[:, last:count], z[:, last:count]], axis=0)
            right = jnp.concatenate([z, x], axis=0)
            gram[last:count, :] = gram[last:count, :] - lax.dot_general(
                left, right, (((0,), (0,)), ((), ())), precision=HI, preferred_element_type=jnp.float32)
    whole = lax.dot_general(
        inc[...], shift[:, count:], (((0,), (0,)), ((), ())), precision=HI, preferred_element_type=jnp.float32)
    mine = whole[members:2 * members, :members]
    mine = mine + (iota(mine.shape, 0) == iota(mine.shape, 1)).astype(jnp.float32)
    tall, broad = high_ref.shape
    down = (iota((tall, members), 0) // SUB == iota((tall, members), 1)).astype(jnp.float32)
    over = (iota((members, broad), 1) // SUB == iota((members, broad), 0)).astype(jnp.float32)
    spread = jnp.dot(jnp.dot(down, mine, precision=HI), over, precision=HI)
    spread = jnp.where(iota((tall, broad), 0) % SUB == iota((tall, broad), 1) % SUB, spread, 0.0)
    high = spread.astype(jnp.bfloat16)
    high_ref[...] = high
    low_ref[...] = (spread - high.astype(jnp.float32)).astype(jnp.bfloat16)


def run_filter(order, pieces, obs_value, obs_error, wide, group=64):
    here, count = pieces[0].shape
    members = here * len(pieces)
    lanes = count + 2 * members
    smem = pl.BlockSpec(memory_space=pltpu.SMEM)
    vmem = pl.BlockSpec(memory_space=pltpu.VMEM)
    spread = jax.ShapeDtypeStruct((members * SUB, members * SUB), jnp.bfloat16)
    return pl.pallas_call(
        functools.partial(filter_kernel, members=members, group=group),
        out_shape=(spread, spread),
        in_specs=[smem] * 4 + [vmem] * 5,
        out_specs=(vmem, vmem),
        scratch_shapes=[
            pltpu.VMEM((members, count), jnp.float32),
            pltpu.VMEM((count, lanes), jnp.float32),
            pltpu.VMEM((count, lanes), jnp.float32),
            pltpu.VMEM((count, lanes), jnp.float32),
            pltpu.VMEM((count, 128), jnp.float32),
            pltpu.VMEM((8, count), jnp.float32),
        ],
        compiler_params=pltpu.CompilerParams(vmem_limit_bytes=32 * 2**20),
    )(order, obs_value, obs_error, jnp.sqrt(obs_error), *pieces, wide)


def wide_weights(observation_row, localize, own, rows_here, members):
    owner = observation_row // rows_here
    tiles = localize.shape[0]
    hot = (owner[None, :] == jnp.arange(tiles, dtype=jnp.int32)[:, None]).astype(jnp.float32)
    across = lax.dot_general(localize, hot, (((0,), (0,)), ((), ())), precision=HI)
    count = owner.shape[0]
    return jnp.concatenate(
        [across, jnp.broadcast_to(own[:, None], (count, members)), jnp.zeros((count, members), jnp.float32)], axis=1)


def product(high, low, cells):
    both = jnp.concatenate([high, low], axis=0)
    tall = high.shape[0]
    top = cells.astype(jnp.bfloat16)
    rest = (cells - top.astype(jnp.float32)).astype(jnp.bfloat16)
    first = jnp.dot(both, top, preferred_element_type=jnp.float32)
    second = jnp.dot(high, rest, preferred_element_type=jnp.float32)
    return first[:tall] + (first[tall:] + second)


def gathered_kernel(mem_ref, high_ref, low_ref, cells_ref, out_ref):
    here = out_ref.shape[0]
    mine = pl.ds(pl.multiple_of(mem_ref[0] * here * SUB, here * SUB), here * SUB)
    high, low = high_ref[mine, :], low_ref[mine, :]
    for f in range(out_ref.shape[1]):
        for r in range(out_ref.shape[3]):
            cells = cells_ref[:, f, r].reshape(-1, cells_ref.shape[-1])
            out_ref[:, f, :, r, :] = product(high, low, cells).reshape(here, SUB, -1)


def update_gathered(mem_pos, high, low, cells, all_fields):
    members, fields, rows, levels, width = cells.shape
    here = members // 4
    full = pl.BlockSpec(high.shape, lambda i: (0, 0))
    return pl.pallas_call(
        gathered_kernel,
        grid=(levels // SUB,),
        out_shape=jax.ShapeDtypeStruct((here, all_fields, levels, rows, width), jnp.float32),
        in_specs=[
            pl.BlockSpec(memory_space=pltpu.SMEM), full, full,
            pl.BlockSpec((members, fields, rows, SUB, width), lambda i: (0, 0, 0, i, 0)),
        ],
        out_specs=pl.BlockSpec((here, fields, SUB, rows, width), lambda i: (0, 0, i, 0, 0)),
        compiler_params=pltpu.CompilerParams(vmem_limit_bytes=40 * 2**20),
    )(mem_pos.reshape(1), high, low, cells)


def piece_kernel(high_ref, low_ref, cells_ref, out_ref):
    groups, here, fields, _, width = cells_ref.shape
    cells = jnp.concatenate([cells_ref[:, :, f].reshape(-1, width) for f in range(fields)], axis=1)
    total = product(high_ref[...], low_ref[...], cells)
    for f in range(fields):
        out_ref[:, :, f] = total[:, f * width:(f + 1) * width].reshape(groups, here, SUB, width)


def update_piece(high, low, cells):
    groups, here, fields, levels, width = cells.shape
    full = pl.BlockSpec(high.shape, lambda i: (0, 0))
    block = pl.BlockSpec((groups, here, fields, SUB, width), lambda i: (0, 0, 0, i, 0))
    return pl.pallas_call(
        piece_kernel,
        grid=(levels // SUB,),
        out_shape=jax.ShapeDtypeStruct(cells.shape, jnp.float32),
        in_specs=[full, full, block],
        out_specs=block,
        compiler_params=pltpu.CompilerParams(vmem_limit_bytes=40 * 2**20),
    )(high, low, cells)


def join_kernel(back_ref, sofar_ref, out_ref):
    half = back_ref.shape[-1]
    for piece in range(back_ref.shape[0]):
        r, h = piece // 2, piece % 2
        out_ref[:, :, :, r, h * half:(h + 1) * half] = back_ref[piece]


def join(back, sofar):
    pieces, here, fields, levels, half = back.shape
    part = 8
    place = sofar.shape[1] // fields - 1
    return pl.pallas_call(
        join_kernel,
        grid=(here // part,),
        out_shape=jax.ShapeDtypeStruct(sofar.shape, jnp.float32),
        in_specs=[
            pl.BlockSpec((pieces, part, fields, levels, half), lambda m: (0, m, 0, 0, 0)),
            pl.BlockSpec(memory_space=pl.ANY),
        ],
        out_specs=pl.BlockSpec((part, fields) + sofar.shape[2:], lambda m: (m, place, 0, 0, 0)),
        input_output_aliases={1: 0},
    )(back, sofar)


def after(value, *others):
    return lax.optimization_barrier((value,) + others)[0]


def on_device(
    ensemble,
    courant,
    diffusion,
    observation_row,
    observation_column,
    observation_field,
    observation_level,
    obs_value,
    obs_error,
    localize,
):
    members_here, fields, levels, rows_here, width = ensemble.shape
    tiles = lax.axis_size("tile")
    groups = lax.axis_size("mem")
    ens_size = members_here * groups
    tile_pos = lax.axis_index("tile")
    onward = [(i, (i + 1) % tiles) for i in range(tiles)]
    backward = [((i + 1) % tiles, i) for i in range(tiles)]
    start = jnp.transpose(ensemble, (0, 1, 3, 2, 4))
    flow = jnp.transpose(courant, (0, 2, 1, 3))
    spread = jnp.broadcast_to(diffusion[:, :, None], (fields, levels, width))
    own = lax.dynamic_slice_in_dim(localize, tile_pos, 1, 0)[0]
    wide = wide_weights(observation_row, localize, own, rows_here, ens_size)

    mem_pos = lax.axis_index("mem")
    order = lax.rem(mem_pos - jnp.arange(groups, dtype=jnp.int32) + groups, groups)

    def shifted(array, by):
        return lax.ppermute(array, "tile", [(i, (i + by) % tiles) for i in range(tiles)])

    def step(cells, f, into=None, split=False, wait=()):
        below, above = shifted(cells, 1), shifted(cells, -1)
        if wait:
            below = after(below, *wait)
        return forecast_step(cells, below, above, flow, spread, f, into, split)

    middle = [step(start[:, f:f + 1], f) for f in range(fields)]

    def last_step(fields_of, split, wait):
        whole = None
        for place, f in enumerate(fields_of):
            whole = step(middle[f], f, (len(fields_of), place, whole), split, wait)
        return whole

    whole = last_step(GROUPS[0], False, middle)
    split = last_step(GROUPS[1], True, (whole,))
    gathered = lax.all_gather(after(whole, split), "mem", axis=0, tiled=True)
    swapped = lax.all_to_all(split, "mem", 0, 0, tiled=True)
    seen = sample(
        whole, split, tile_pos, observation_row, observation_column, observation_field, observation_level
    )
    for bit in (1, 2, 4, 8, 16, 32):
        seen = seen + lax.ppermute(seen, "tile", [(i, i ^ bit) for i in range(tiles)])
    pieces = [seen] + [lax.ppermute(seen, "mem", [(i, (i + d) % groups) for i in range(groups)]) for d in range(1, groups)]
    high, low = run_filter(order, pieces, obs_value, obs_error, wide)
    back = lax.all_to_all(update_piece(high, low, swapped), "mem", 0, 0, tiled=True)
    result = update_gathered(mem_pos, high, low, gathered, fields)
    return join(back, result)


def solution(mesh):
    placed = (
        P("mem", None, None, "tile", None),
        P(None, None, "tile", None),
        P(),
        P(),
        P(),
        P(),
        P(),
        P(),
        P(),
        P(),
    )
    return jax.shard_map(
        on_device,
        mesh=mesh,
        in_specs=placed,
        out_specs=P("mem", None, None, "tile", None),
        check_vma=False,
    )
```

```python
import functools

import jax
import jax.numpy as jnp
from jax import lax
from jax.experimental import pallas as pl
from jax.experimental.pallas import tpu as pltpu
from jax.sharding import PartitionSpec as P

STEPS = 2
HI = lax.Precision.HIGHEST
BLK = 8
SUB = 8
GROUPS = ((0, 1), (2, 3))


def iota(shape, dim):
    return lax.broadcasted_iota(jnp.int32, shape, dim)


def step_kernel(split, cells_ref, below_ref, above_ref, courant_ref, spread_ref, *refs):
    out_ref = refs[-1]
    width = cells_ref.shape[-1]
    spread = spread_ref[0]
    for r in range(2):
        along, across = courant_ref[0, r], courant_ref[1, r]
        middle = 1.0 - 4.0 * spread
        up, down, two = spread - along * (2.0 / 3.0), spread + along * (2.0 / 3.0), along * (1.0 / 12.0)
        right, left, far = spread - across * (2.0 / 3.0), spread + across * (2.0 / 3.0), across * (1.0 / 12.0)
        for member in range(cells_ref.shape[0]):
            rows = [ref[member, 0, i] for ref in (below_ref, cells_ref, above_ref) for i in range(2)]
            centre = rows[2 + r]
            value = (
                (middle * centre + two * (rows[4 + r] - rows[r]))
                + (up * rows[3 + r] + down * rows[1 + r])
                + (right * pltpu.roll(centre, width - 1, 1) + left * pltpu.roll(centre, 1, 1))
                + far * (pltpu.roll(centre, width - 2, 1) - pltpu.roll(centre, 2, 1))
            )
            if split:
                for half in range(2):
                    out_ref[2 * r + half, member, 0] = value[:, half * (width // 2):(half + 1) * (width // 2)]
            else:
                out_ref[member, 0, r] = value


def forecast_step(cells, below, above, courant, spread, field, into=None, split=False):
    count, _, rows, levels, width = below.shape
    part = 8
    block = pl.BlockSpec((part, 1, rows, levels, width), lambda m: (m, 0, 0, 0, 0))
    fields, place, sofar = into or (1, 0, None)
    more = [] if sofar is None else [sofar]
    if split:
        shape = (2 * rows, count, fields, levels, width // 2)
        out_block = pl.BlockSpec((2 * rows, part, 1, levels, width // 2), lambda m: (0, m, place, 0, 0))
    else:
        shape = (count, fields, rows, levels, width)
        out_block = pl.BlockSpec((part, 1, rows, levels, width), lambda m: (m, place, 0, 0, 0))
    return pl.pallas_call(
        functools.partial(step_kernel, split),
        grid=(count // part,),
        out_shape=jax.ShapeDtypeStruct(shape, jnp.float32),
        in_specs=[
            block,
            block,
            block,
            pl.BlockSpec((2, rows, levels, width), lambda m: (0, 0, 0, 0)),
            pl.BlockSpec((1, levels, width), lambda m: (field, 0, 0)),
        ] + [pl.BlockSpec(memory_space=pl.ANY) for _ in more],
        out_specs=out_block,
        input_output_aliases={5: 0} if more else {},
        cost_estimate=pl.CostEstimate(flops=below.size, bytes_accessed=below.size, transcendentals=0),
    )(cells, below, above, courant, spread, *more)


def sample_kernel(tile_ref, row_ref, column_ref, field_ref, level_ref, whole_ref, split_ref, out_ref, mine):
    members, count = out_ref.shape
    early, rows_here = whole_ref.shape[1:3]
    first = tile_ref[0] * rows_here
    out_ref[...] = jnp.zeros(out_ref.shape, jnp.float32)
    line = iota((members, SUB, 128), 1)
    place = iota((members, 128), 1)

    def look(k, found):
        mine[found] = k
        row = row_ref[k] - first
        return found + ((row >= 0) & (row < rows_here)).astype(jnp.int32)

    found = lax.fori_loop(0, count, look, jnp.int32(0), unroll=8)

    def one(index, carry):
        k = mine[index]
        row = row_ref[k] - first
        level = level_ref[k]
        column = column_ref[k]
        field = field_ref[k]
        level_base = pl.multiple_of((level // SUB) * SUB, SUB)
        column_base = pl.multiple_of((column // 128) * 128, 128)
        target = pl.multiple_of((k // 128) * 128, 128)

        def put(seen):
            value = jnp.sum(jnp.where(line == level - level_base, seen, 0.0), axis=1)
            value = pltpu.roll(value, lax.rem(k - column + 512, 128), 1)
            kept = out_ref[:, pl.ds(target, 128)]
            out_ref[:, pl.ds(target, 128)] = jnp.where(place == k - target, value, kept)

        @pl.when(field < early)
        def _():
            put(whole_ref[:, field, row, pl.ds(level_base, SUB), pl.ds(column_base, 128)])

        @pl.when(field >= early)
        def _():
            put(split_ref[2 * row + column // 128, :, field - early, pl.ds(level_base, SUB), :])

        return carry

    lax.fori_loop(0, found, one, 0)


def sample(whole, split, tile_pos, row, column, field, level):
    smem = pl.BlockSpec(memory_space=pltpu.SMEM)
    vmem = pl.BlockSpec(memory_space=pltpu.VMEM)
    return pl.pallas_call(
        sample_kernel,
        out_shape=jax.ShapeDtypeStruct((whole.shape[0], row.shape[0]), jnp.float32),
        in_specs=[smem] * 5 + [vmem] * 2,
        out_specs=vmem,
        scratch_shapes=[pltpu.SMEM((row.shape[0] + 1,), jnp.int32)],
        compiler_params=pltpu.CompilerParams(vmem_limit_bytes=32 * 2**20),
    )(tile_pos.reshape(1), row, column, field, level, whole, split)


def filter_kernel(order_ref, obs_ref, err_ref, root_ref, raw_0, raw_1, raw_2, raw_3, wide_ref, high_ref, low_ref, joined, gram, shift, slope, inc, mean_ref, *, members, group):
    count = raw_0.shape[1]
    lanes = gram.shape[1]
    freedom = members - 1.0
    here = raw_0.shape[0]
    for j, piece in enumerate((raw_0, raw_1, raw_2, raw_3)):
        joined[pl.ds(pl.multiple_of(order_ref[j] * here, here), here), :] = piece[...]
    raw = jnp.transpose(joined[...])
    centre = jnp.sum(raw, axis=1, keepdims=True) / members
    anomaly = raw - centre
    mean_ref[...] = jnp.transpose(jnp.broadcast_to(centre, (count, 8 * 16)))[:8, :]
    gram[:, :count] = lax.dot_general(
        anomaly, anomaly * (1.0 / freedom), (((1,), (1,)), ((), ())), precision=HI,
        preferred_element_type=jnp.float32)
    gram[:, count:] = jnp.concatenate([anomaly * (1.0 / freedom), anomaly], axis=1)

    def lift(array, row, column):
        return jnp.broadcast_to(jnp.broadcast_to(array[:, column:column + 1], (BLK, 128))[row:row + 1, :], (BLK, 128))

    def block(position, first, last):
        base = pl.multiple_of(position * BLK, BLK)
        tile = pl.multiple_of((base // 128) * 128, 128)
        back = lax.rem(128 - lax.rem(base, 128), 128)
        panel = gram[pl.ds(base, BLK), :]
        weight = wide_ref[pl.ds(base, BLK), :]
        corner = pltpu.roll(gram[pl.ds(base, BLK), pl.ds(tile, 128)], back, 1)
        corner_w = pltpu.roll(wide_ref[pl.ds(base, BLK), pl.ds(tile, 128)], back, 1)
        corner_m = pltpu.roll(mean_ref[:, pl.ds(tile, 128)], back, 1)
        cell = {(k, l): lift(corner, l, k) for l in range(BLK) for k in range(l, BLK)}
        means = [jnp.broadcast_to(corner_m[:, k:k + 1], (BLK, 128)) for k in range(BLK)]
        rows = [[jnp.broadcast_to(panel[k:k + 1, c:c + 128], (BLK, 128)) for c in range(0, lanes, 128)] for k in range(BLK)]
        line = lax.broadcasted_iota(jnp.int32, (BLK, 128), 0)
        tiles = range(lanes // 128)
        keep_x = [jnp.zeros((BLK, 128), jnp.float32) for _ in tiles]
        keep_z = [jnp.zeros((BLK, 128), jnp.float32) for _ in tiles]
        keep_g = jnp.zeros((BLK, 128), jnp.float32)
        mean_row = [mean_ref[:, c:c + 128] for c in range(0, count, 128)]
        for i in range(BLK):
            err = err_ref[base + i]
            root = root_ref[base + i]
            v = cell[i, i]
            s = v + err
            t = lax.rsqrt(s)
            e = 1.0 / (s + root * (s * t))
            h = 0.5 * (e * v)
            d = (obs_ref[base + i] - means[i]) * (t * t)
            xs, zs = {}, {}
            for k in range(i + 1, BLK):
                q = cell[k, i]
                xs[k] = lift(corner_w, i, k) * q
                zs[k] = e * (q - h * xs[k])
                means[k] = means[k] + d * xs[k]
            for l in range(i + 1, BLK):
                for k in range(l, BLK):
                    cell[k, l] = cell[k, l] - xs[k] * zs[l] - zs[k] * xs[l]
            for c in range(lanes // 128):
                q = rows[i][c]
                x = jnp.broadcast_to(weight[i:i + 1, 128 * c:128 * c + 128], (BLK, 128)) * q
                z = e * (q - h * x)
                for k in range(i + 1, BLK):
                    rows[k][c] = rows[k][c] - xs[k] * z - zs[k] * x
                keep_x[c] = jnp.where(line == i, x, keep_x[c])
                keep_z[c] = jnp.where(line == i, z, keep_z[c])
                if c < count // 128:
                    mean_row[c] = mean_row[c] + d * x
                if c == lanes // 128 - 1:
                    keep_g = jnp.where(line == i, d - e * q, keep_g)
        for c in range(count // 128):
            mean_ref[:, 128 * c:128 * c + 128] = mean_row[c]
        x = jnp.concatenate(keep_x, axis=1)
        z = jnp.concatenate(keep_z, axis=1)
        shift[pl.ds(base, BLK), :] = x
        slope[pl.ds(base, BLK), :] = z
        inc[pl.ds(base, BLK), :] = keep_g
        left = jnp.concatenate([x[:, first:last], z[:, first:last]], axis=0)
        right = jnp.concatenate([z, x], axis=0)
        left_top, right_top = left.astype(jnp.bfloat16), right.astype(jnp.bfloat16)
        left_rest = (left - left_top.astype(jnp.float32)).astype(jnp.bfloat16)
        right_rest = (right - right_top.astype(jnp.float32)).astype(jnp.bfloat16)
        gram[first:last, :] = gram[first:last, :] - lax.dot_general(
            jnp.concatenate([left_top, left_rest, left_top], axis=0),
            jnp.concatenate([right_top, right_top, right_rest], axis=0),
            (((0,), (0,)), ((), ())), preferred_element_type=jnp.float32)

    for first in range(0, count, group):
        last = first + group

        def body(position, carry):
            block(position, first, last)
            return carry

        lax.fori_loop(first // BLK, last // BLK, body, 0)
        if last < count:
            x = shift[first:last, :]
            z = slope[first:last, :]
            left = jnp.concatenate([x[:, last:count], z[:, last:count]], axis=0)
            right = jnp.concatenate([z, x], axis=0)
            gram[last:count, :] = gram[last:count, :] - lax.dot_general(
                left, right, (((0,), (0,)), ((), ())), precision=HI, preferred_element_type=jnp.float32)
    whole = lax.dot_general(
        inc[...], shift[:, count:], (((0,), (0,)), ((), ())), precision=HI, preferred_element_type=jnp.float32)
    mine = whole[members:2 * members, :members]
    mine = mine + (iota(mine.shape, 0) == iota(mine.shape, 1)).astype(jnp.float32)
    tall, broad = high_ref.shape
    down = (iota((tall, members), 0) // SUB == iota((tall, members), 1)).astype(jnp.bfloat16)
    over = (iota((members, broad), 1) // SUB == iota((members, broad), 0)).astype(jnp.bfloat16)
    level = iota((tall, broad), 0) % SUB == iota((tall, broad), 1) % SUB
    top = mine.astype(jnp.bfloat16)
    rest = (mine - top.astype(jnp.float32)).astype(jnp.bfloat16)
    for part, ref in ((top, high_ref), (rest, low_ref)):
        rows = jnp.dot(down, part, preferred_element_type=jnp.float32).astype(jnp.bfloat16)
        spread = jnp.dot(rows, over, preferred_element_type=jnp.float32)
        ref[...] = jnp.where(level, spread, 0.0).astype(jnp.bfloat16)


def run_filter(order, pieces, obs_value, obs_error, wide, group=64):
    here, count = pieces[0].shape
    members = here * len(pieces)
    lanes = count + 2 * members
    smem = pl.BlockSpec(memory_space=pltpu.SMEM)
    vmem = pl.BlockSpec(memory_space=pltpu.VMEM)
    spread = jax.ShapeDtypeStruct((members * SUB, members * SUB), jnp.bfloat16)
    return pl.pallas_call(
        functools.partial(filter_kernel, members=members, group=group),
        out_shape=(spread, spread),
        in_specs=[smem] * 4 + [vmem] * 5,
        out_specs=(vmem, vmem),
        scratch_shapes=[
            pltpu.VMEM((members, count), jnp.float32),
            pltpu.VMEM((count, lanes), jnp.float32),
            pltpu.VMEM((count, lanes), jnp.float32),
            pltpu.VMEM((count, lanes), jnp.float32),
            pltpu.VMEM((count, 128), jnp.float32),
            pltpu.VMEM((8, count), jnp.float32),
        ],
        compiler_params=pltpu.CompilerParams(vmem_limit_bytes=32 * 2**20),
    )(order, obs_value, obs_error, jnp.sqrt(obs_error), *pieces, wide)


def wide_weights(observation_row, localize, own, rows_here, members):
    owner = observation_row // rows_here
    tiles = localize.shape[0]
    hot = (owner[None, :] == jnp.arange(tiles, dtype=jnp.int32)[:, None]).astype(jnp.float32)
    across = lax.dot_general(localize, hot, (((0,), (0,)), ((), ())), precision=HI)
    count = owner.shape[0]
    return jnp.concatenate(
        [across, jnp.broadcast_to(own[:, None], (count, members)), jnp.zeros((count, members), jnp.float32)], axis=1)


def product(high, low, cells):
    both = jnp.concatenate([high, low], axis=0)
    tall = high.shape[0]
    top = cells.astype(jnp.bfloat16)
    rest = (cells - top.astype(jnp.float32)).astype(jnp.bfloat16)
    first = jnp.dot(both, top, preferred_element_type=jnp.float32)
    second = jnp.dot(high, rest, preferred_element_type=jnp.float32)
    return first[:tall] + (first[tall:] + second)


def gathered_kernel(mem_ref, high_ref, low_ref, cells_ref, out_ref):
    here = out_ref.shape[0]
    mine = pl.ds(pl.multiple_of(mem_ref[0] * here * SUB, here * SUB), here * SUB)
    high, low = high_ref[mine, :], low_ref[mine, :]
    for f in range(out_ref.shape[1]):
        for r in range(out_ref.shape[3]):
            cells = cells_ref[:, f, r].reshape(-1, cells_ref.shape[-1])
            out_ref[:, f, :, r, :] = product(high, low, cells).reshape(here, SUB, -1)


def update_gathered(mem_pos, high, low, cells, all_fields):
    members, fields, rows, levels, width = cells.shape
    here = members // 4
    full = pl.BlockSpec(high.shape, lambda i: (0, 0))
    return pl.pallas_call(
        gathered_kernel,
        grid=(levels // SUB,),
        out_shape=jax.ShapeDtypeStruct((here, all_fields, levels, rows, width), jnp.float32),
        in_specs=[
            pl.BlockSpec(memory_space=pltpu.SMEM), full, full,
            pl.BlockSpec((members, fields, rows, SUB, width), lambda i: (0, 0, 0, i, 0)),
        ],
        out_specs=pl.BlockSpec((here, fields, SUB, rows, width), lambda i: (0, 0, i, 0, 0)),
        compiler_params=pltpu.CompilerParams(vmem_limit_bytes=40 * 2**20),
    )(mem_pos.reshape(1), high, low, cells)


def piece_kernel(high_ref, low_ref, cells_ref, out_ref):
    groups, here, fields, _, width = cells_ref.shape
    cells = jnp.concatenate([cells_ref[:, :, f].reshape(-1, width) for f in range(fields)], axis=1)
    total = product(high_ref[...], low_ref[...], cells)
    for f in range(fields):
        out_ref[:, :, f] = total[:, f * width:(f + 1) * width].reshape(groups, here, SUB, width)


def update_piece(high, low, cells):
    groups, here, fields, levels, width = cells.shape
    full = pl.BlockSpec(high.shape, lambda i: (0, 0))
    block = pl.BlockSpec((groups, here, fields, SUB, width), lambda i: (0, 0, 0, i, 0))
    return pl.pallas_call(
        piece_kernel,
        grid=(levels // SUB,),
        out_shape=jax.ShapeDtypeStruct(cells.shape, jnp.float32),
        in_specs=[full, full, block],
        out_specs=block,
        compiler_params=pltpu.CompilerParams(vmem_limit_bytes=40 * 2**20),
    )(high, low, cells)


def join_kernel(back_ref, sofar_ref, out_ref):
    half = back_ref.shape[-1]
    for piece in range(back_ref.shape[0]):
        r, h = piece // 2, piece % 2
        out_ref[:, :, :, r, h * half:(h + 1) * half] = back_ref[piece]


def join(back, sofar):
    pieces, here, fields, levels, half = back.shape
    part = 8
    place = sofar.shape[1] // fields - 1
    return pl.pallas_call(
        join_kernel,
        grid=(here // part,),
        out_shape=jax.ShapeDtypeStruct(sofar.shape, jnp.float32),
        in_specs=[
            pl.BlockSpec((pieces, part, fields, levels, half), lambda m: (0, m, 0, 0, 0)),
            pl.BlockSpec(memory_space=pl.ANY),
        ],
        out_specs=pl.BlockSpec((part, fields) + sofar.shape[2:], lambda m: (m, place, 0, 0, 0)),
        input_output_aliases={1: 0},
    )(back, sofar)


def after(value, *others):
    return lax.optimization_barrier((value,) + others)[0]


def on_device(
    ensemble,
    courant,
    diffusion,
    observation_row,
    observation_column,
    observation_field,
    observation_level,
    obs_value,
    obs_error,
    localize,
):
    members_here, fields, levels, rows_here, width = ensemble.shape
    tiles = lax.axis_size("tile")
    groups = lax.axis_size("mem")
    ens_size = members_here * groups
    tile_pos = lax.axis_index("tile")
    onward = [(i, (i + 1) % tiles) for i in range(tiles)]
    backward = [((i + 1) % tiles, i) for i in range(tiles)]
    start = jnp.transpose(ensemble, (0, 1, 3, 2, 4))
    flow = jnp.transpose(courant, (0, 2, 1, 3))
    spread = jnp.broadcast_to(diffusion[:, :, None], (fields, levels, width))
    own = lax.dynamic_slice_in_dim(localize, tile_pos, 1, 0)[0]
    wide = wide_weights(observation_row, localize, own, rows_here, ens_size)

    mem_pos = lax.axis_index("mem")
    order = lax.rem(mem_pos - jnp.arange(groups, dtype=jnp.int32) + groups, groups)

    def shifted(array, by):
        return lax.ppermute(array, "tile", [(i, (i + by) % tiles) for i in range(tiles)])

    def step(cells, f, into=None, split=False, wait=()):
        below, above = shifted(cells, 1), shifted(cells, -1)
        if wait:
            below = after(below, *wait)
        return forecast_step(cells, below, above, flow, spread, f, into, split)

    middle = [step(start[:, f:f + 1], f) for f in range(fields)]

    def last_step(fields_of, split, wait):
        whole = None
        for place, f in enumerate(fields_of):
            whole = step(middle[f], f, (len(fields_of), place, whole), split, wait)
        return whole

    whole = last_step(GROUPS[0], False, middle)
    split = last_step(GROUPS[1], True, (whole,))
    gathered = lax.all_gather(after(whole, split), "mem", axis=0, tiled=True)
    swapped = lax.all_to_all(split, "mem", 0, 0, tiled=True)
    seen = sample(
        whole, split, tile_pos, observation_row, observation_column, observation_field, observation_level
    )
    for bit in (1, 2, 4, 8, 16, 32):
        seen = seen + lax.ppermute(seen, "tile", [(i, i ^ bit) for i in range(tiles)])
    pieces = [seen] + [lax.ppermute(seen, "mem", [(i, (i + d) % groups) for i in range(groups)]) for d in range(1, groups)]
    high, low = run_filter(order, pieces, obs_value, obs_error, wide)
    back = lax.all_to_all(update_piece(high, low, swapped), "mem", 0, 0, tiled=True)
    result = update_gathered(mem_pos, high, low, gathered, fields)
    return join(back, result)


def solution(mesh):
    placed = (
        P("mem", None, None, "tile", None),
        P(None, None, "tile", None),
        P(),
        P(),
        P(),
        P(),
        P(),
        P(),
        P(),
        P(),
    )
    return jax.shard_map(
        on_device,
        mesh=mesh,
        in_specs=placed,
        out_specs=P("mem", None, None, "tile", None),
        check_vma=False,
    )
```
